32 devices in a mesh: dp: 8 (over y, x, core), ctx: 4 (over z).
Axes of the slice: x: 2, y: 2, z: 4, core: 2. Of those that a mesh axis runs over, the one named last changes fastest.
Arguments:
- tokens: bfloat16 [8, 2048, 1088], P('dp', 'ctx'), may hold values from -6 to 6
- first_gain: bfloat16 [1088], P('dp'), may hold values from 0.5 to 1.5
- first_shift: bfloat16 [1088], P('dp'), may hold values from -3 to 3
- qkv_weight: bfloat16 [1088, 3264], P('dp'), may hold values from -0.1875 to 0.1875
- query_bias: bfloat16 [1088], P('dp'), may hold values from -3 to 3
- value_bias: bfloat16 [1088], P('dp'), may hold values from -3 to 3
- proj_weight: bfloat16 [1088, 1088], P('dp'), may hold values from -1.5 to 1.5
- proj_bias: bfloat16 [1088], P('dp'), may hold values from -3 to 3
- second_gain: bfloat16 [1088], P('dp'), may hold values from 0.5 to 1.5
- second_shift: bfloat16 [1088], P('dp'), may hold values from -3 to 3
- up_weight: bfloat16 [1088, 4352], P('dp'), may hold values from -0.1875 to 0.1875
- up_bias: bfloat16 [4352], P('dp'), may hold values from -3 to 3
- down_weight: bfloat16 [4352, 1088], P('dp'), may hold values from -0.09375 to 0.09375
- down_bias: bfloat16 [1088], P('dp'), may hold values from -3 to 3
- block_order: int32 [8], replicated, may hold values from 0 to 7, each once
- cotangent: bfloat16 [8, 2048, 1088], P('dp', 'ctx'), may hold values from -6 to 6
Outputs:
- output: bfloat16 [8, 2048, 1088], P('dp', 'ctx')
- grad_tokens: bfloat16 [8, 2048, 1088], P('dp', 'ctx')
- grad_first_gain: float32 [1088], P('dp')
- grad_first_shift: float32 [1088], P('dp')
- grad_qkv_weight: float32 [1088, 3264], P('dp')
- grad_query_bias: float32 [1088], P('dp')
- grad_value_bias: float32 [1088], P('dp')
- grad_proj_weight: float32 [1088, 1088], P('dp')
- grad_proj_bias: float32 [1088], P('dp')
- grad_second_gain: float32 [1088], P('dp')
- grad_second_shift: float32 [1088], P('dp')
- grad_up_weight: float32 [1088, 4352], P('dp')
- grad_up_bias: float32 [4352], P('dp')
- grad_down_weight: float32 [4352, 1088], P('dp')
- grad_down_bias: float32 [1088], P('dp')
The draws below stay inside these ranges and needn't reach their ends.
Inputs may be any that keep to these rules, and one draw needn't show every extreme that they name: Each of the 8 blocks of a sequence appears once; the rows b * 256 to (b + 1) * 256 - 1 of dimension 1 hold the positions from block_order[b] 256 on, the same for every sequence.
All inputs are finite; a program needn't handle non-finite values.
Results may differ from the reference program's by a relative error of at most 0.018.
Values may be sent and summed in bfloat16 or wider, within the bound.
A program may use at most 384 MiB of HBM per device.

```python
import math
import jax
import jax.numpy as jnp
from jax import lax

D = 1088
HEADS = 17
FF = 4352
SEQ_LEN = 2048
BLOCKS = 8
BLK = 256
SEQS = 8


def levels(rng, dims, split, low, top_value):
    def one(dim, parts):
        heights = jax.random.uniform(jax.random.fold_in(jax.random.fold_in(rng, 6), dim), (parts,), jnp.float32, low / len(split), top_value / len(split))
        return jnp.repeat(jnp.exp(heights), dims[dim] // parts).reshape((-1,) + (1,) * (len(dims) - dim - 1))

    gain = one(*split[0])
    for cut in split[1:]:
        gain = gain * one(*cut)
    return gain


def noise(own_key, dims, scale, reach, shards=(), kind=jnp.bfloat16):
    drawn = jax.random.normal(own_key, dims, jnp.float32) * scale
    if len(shards) > 0:
        drawn = levels(own_key, dims, shards, -0.22, 0.18) * drawn
    return jnp.clip(drawn, min=-reach, max=reach).astype(kind)


def setup_inputs(seed: int = 0) -> dict:
    splits = jax.random.split(jax.random.key(seed), 17)
    tokens = noise(splits[0], (SEQS, SEQ_LEN, D), 1.0, 6.0, ((0, 8), (1, 4)))
    first_gain = jnp.clip(1.0 + 0.1 * jax.random.normal(splits[1], (D,), jnp.float32), 0.5, 1.5).astype(jnp.bfloat16)
    first_shift = noise(splits[2], (D,), 0.5, 3.0, ((0, 8),))
    qkv_weight = noise(splits[3], (D, 3 * D), D ** -0.5, 0.1875, ((0, 8),))
    query_bias = noise(splits[4], (D,), 0.5, 3.0, ((0, 8),))
    value_bias = noise(splits[5], (D,), 0.5, 3.0, ((0, 8),))
    proj_weight = noise(splits[6], (D, D), (D // 64) ** -0.5, 1.5, ((0, 8),))
    proj_bias = noise(splits[7], (D,), 0.5, 3.0, ((0, 8),))
    second_gain = jnp.clip(1.0 + 0.1 * jax.random.normal(splits[8], (D,), jnp.float32), 0.5, 1.5).astype(jnp.bfloat16)
    second_shift = noise(splits[9], (D,), 0.5, 3.0, ((0, 8),))
    up_weight = noise(splits[10], (D, FF), D ** -0.5, 0.1875, ((0, 8),))
    up_bias = noise(splits[11], (FF,), 0.5, 3.0, ((0, 8),))
    down_weight = noise(splits[12], (FF, D), FF ** -0.5, 0.09375, ((0, 8),))
    down_bias = noise(splits[13], (D,), 0.5, 3.0, ((0, 8),))
    block_order = jax.random.permutation(splits[14], BLOCKS).astype(jnp.int32)
    cotangent = noise(splits[15], (SEQS, SEQ_LEN, D), 1.0, 6.0, ((0, 8), (1, 4)))
    return {"tokens": tokens, "first_gain": first_gain, "first_shift": first_shift, "qkv_weight": qkv_weight, "query_bias": query_bias, "value_bias": value_bias, "proj_weight": proj_weight, "proj_bias": proj_bias, "second_gain": second_gain, "second_shift": second_shift, "up_weight": up_weight, "up_bias": up_bias, "down_weight": down_weight, "down_bias": down_bias, "block_order": block_order, "cotangent": cotangent}


@jax.custom_vjp
def low(v):
    return lax.optimization_barrier(v.astype(jnp.bfloat16)).astype(jnp.float32)

@jax.custom_vjp
def low_back(v):
    return v

def low_keep(v):
    return (low(v), None)

def low_pass(kept, grad):
    return (grad,)

def back_keep(v):
    return (v, None)

def back_low(kept, grad):
    return (low(grad),)
low.defvjp(low_keep, low_pass)
low_back.defvjp(back_keep, back_low)
eps = 1e-05
neg_large = -1e+30

def product(left, right):
    return jnp.dot(left, right, precision=lax.Precision.HIGHEST, preferred_element_type=jnp.float32)

def layer_norm(values, norm_gain, norm_shift):
    average = lax.optimization_barrier(jnp.mean(values, axis=-1, keepdims=True))
    centered = values - average
    spread = lax.optimization_barrier(jnp.mean(centered * centered, axis=-1, keepdims=True))
    return centered * lax.rsqrt(spread + eps) * norm_gain + norm_shift

def attention(queries, keys, values, visible):
    head_size = D // HEADS
    query_heads = queries.reshape(SEQ_LEN, HEADS, head_size)
    key_heads = keys.reshape(SEQ_LEN, HEADS, head_size)
    value_heads = values.reshape(SEQ_LEN, HEADS, head_size)
    scores = jnp.einsum('qhd,khd->hqk', query_heads, key_heads, precision=lax.Precision.HIGHEST)
    scores = low_back(scores)
    scores = jnp.where(visible[None, :, :], scores, neg_large)
    highest = lax.optimization_barrier(jnp.max(scores, axis=-1, keepdims=True))
    raised = jnp.exp(scores - highest)
    weights = raised / lax.optimization_barrier(jnp.sum(raised, axis=-1, keepdims=True))
    weights = low(weights)
    mixed = jnp.einsum('hqk,khd->qhd', weights, value_heads, precision=lax.Precision.HIGHEST)
    return mixed.reshape(SEQ_LEN, D)

def sequence_forward(sequence, params, visible):
    first_gain, first_shift, qkv_weight, query_bias, value_bias, proj_weight, proj_bias, second_gain, second_shift, up_weight, up_bias, down_weight, down_bias = params
    scale = 1.0 / math.sqrt(D // HEADS)
    normed_one = low(layer_norm(sequence, first_gain, first_shift))
    joined = product(normed_one, qkv_weight)
    queries = low_back(low((joined[:, :D] + query_bias) * scale))
    keys = low_back(low(joined[:, D:2 * D]))
    values = low_back(low(joined[:, 2 * D:] + value_bias))
    attended = low_back(low(attention(queries, keys, values, visible)))
    branch = low_back(product(attended, proj_weight) + proj_bias)
    middle = sequence + branch
    normed_two = low(layer_norm(middle, second_gain, second_shift))
    hidden = low_back(product(normed_two, up_weight) + up_bias)
    active = low(jax.nn.gelu(hidden, approximate=True))
    return middle + product(active, down_weight) + down_bias

def reference(tokens, first_gain, first_shift, qkv_weight, query_bias, value_bias, proj_weight, proj_bias, second_gain, second_shift, up_weight, up_bias, down_weight, down_bias, block_order, cotangent):
    params = tuple((argument.astype(jnp.float32) for argument in (first_gain, first_shift, qkv_weight, query_bias, value_bias, proj_weight, proj_bias, second_gain, second_shift, up_weight, up_bias, down_weight, down_bias)))
    offsets = jnp.arange(BLK, dtype=jnp.int32)
    positions = (block_order.astype(jnp.int32)[:, None] * BLK + offsets[None, :]).reshape(SEQ_LEN)
    visible = positions[:, None] >= positions[None, :]

    def whole(inputs, weights_all):
        per_sequence = jax.checkpoint(lambda sequence: sequence_forward(sequence, weights_all, visible))
        return lax.map(per_sequence, inputs)
    result, pullback = jax.vjp(whole, tokens.astype(jnp.float32), params)
    grad_inputs, grad_params = pullback(cotangent.astype(jnp.float32))
    return (result.astype(jnp.bfloat16), grad_inputs.astype(jnp.bfloat16), grad_params[0], grad_params[1], grad_params[2], grad_params[3], grad_params[4], grad_params[5], grad_params[6], grad_params[7], grad_params[8], grad_params[9], grad_params[10], grad_params[11], grad_params[12])
```

```python
import math

import jax
import jax.numpy as jnp
from jax import lax
from jax.sharding import PartitionSpec as P

HEADS = 17


eps = 1e-05
neg_large = -1e30


def layer_norm(values, norm_gain, norm_shift):
    average = jnp.mean(values, axis=-1, keepdims=True)
    centered = values - average
    spread = jnp.mean(centered * centered, axis=-1, keepdims=True)
    return centered * lax.rsqrt(spread + eps) * norm_gain + norm_shift


def gelu_tanh(values):
    return jax.nn.gelu(values, approximate=True)


def block_positions(block_order, first_row, count, block_rows):
    row_index = first_row + jnp.arange(count, dtype=jnp.int32)
    block_index = row_index // block_rows
    numbers = jnp.arange(block_order.shape[0], dtype=jnp.int32)
    picked = jnp.sum(
        jnp.where(block_index[:, None] == numbers[None, :], block_order[None, :], 0), axis=1
    )
    return picked * block_rows + row_index % block_rows


def swap(values, axis, bit):
    count = lax.axis_size(axis)
    return lax.ppermute(values, axis, [(i, i ^ (1 << bit)) for i in range(count)])


def bit_of(axis, bit):
    return (lax.axis_index(axis) >> bit) & 1


def bits_in(axis):
    return lax.axis_size(axis).bit_length() - 1


def halve(parts, axis, order, wire):
    left = list(range(bits_in(axis)))
    for bit in order:
        low = 1 << left.index(bit)
        left.remove(bit)
        rest = parts.shape[1:]
        view = parts.reshape((parts.shape[0] // (2 * low), 2, low) + rest)
        mine = bit_of(axis, bit)
        sent = lax.dynamic_index_in_dim(view, 1 - mine, 1, keepdims=False).astype(wire)
        kept = lax.dynamic_index_in_dim(view, mine, 1, keepdims=False)
        total = kept.astype(jnp.float32) + swap(sent, axis, bit).astype(jnp.float32)
        parts = total.astype(wire).reshape((-1,) + rest)
    return parts[0]


def double(piece, axis, order):
    have = []
    parts = piece[None]
    for bit in order:
        low = 1 << sum(1 for other in have if other < bit)
        have.append(bit)
        rest = parts.shape[1:]
        other = swap(parts, axis, bit)
        mine = bit_of(axis, bit) == 1
        first = jnp.where(mine, other, parts)
        second = jnp.where(mine, parts, other)
        high = parts.shape[0] // low
        pair = jnp.stack(
            (first.reshape((high, low) + rest), second.reshape((high, low) + rest)), axis=1
        )
        parts = pair.reshape((-1,) + rest)
    return parts


def reduce_matrix(grad, flip):
    dp_count, ctx_count = lax.axis_size("dp"), lax.axis_size("ctx")
    rows, columns = grad.shape
    order = list(range(bits_in("dp")))
    if flip:
        order = order[:1] + order[:0:-1]
    own = rows // dp_count
    shard = halve(grad.reshape(dp_count, own, columns), "dp", order, jnp.bfloat16)
    order = list(range(bits_in("ctx")))
    extra = -own % ctx_count
    if extra:
        shard = jnp.pad(shard, ((0, extra), (0, 0)))
    piece = halve(shard.reshape(ctx_count, -1, columns), "ctx", order, jnp.bfloat16)
    gathered = double(piece, "ctx", order[::-1]).reshape(-1, columns)
    return gathered[:own].astype(jnp.float32)


def reduce_vectors(grads):
    dp_count = lax.axis_size("dp")
    parts = jnp.concatenate([grad.reshape(dp_count, -1) for grad in grads], axis=1)
    total = halve(parts, "dp", list(range(bits_in("dp"))), jnp.float32)
    for bit in range(bits_in("ctx")):
        total = total + swap(total, "ctx", bit)
    sizes = [grad.shape[0] // dp_count for grad in grads]
    return jnp.split(total, [sum(sizes[: i + 1]) for i in range(len(sizes) - 1)])


def gather_vectors(shards):
    joined = jnp.concatenate(shards).astype(jnp.float32)
    parts = double(joined, "dp", list(range(bits_in("dp"))))
    sizes = [shard.shape[0] for shard in shards]
    pieces = jnp.split(parts, [sum(sizes[: i + 1]) for i in range(len(sizes) - 1)], axis=1)
    return [piece.reshape(-1) for piece in pieces]


def per_device(
    tokens,
    first_gain,
    first_shift,
    qkv_weight,
    query_bias,
    value_bias,
    proj_weight,
    proj_bias,
    second_gain,
    second_shift,
    up_weight,
    up_bias,
    down_weight,
    down_bias,
    block_order,
    cotangent,
):
    seq_count, local_rows, width = tokens.shape
    head_count = HEADS
    head_size = width // head_count
    scale = 1.0 / math.sqrt(head_size)
    block_rows = local_rows // 2
    total_rows = seq_count * local_rows
    place_index = lax.axis_index("ctx")
    query_pos = block_positions(block_order, place_index * local_rows, local_rows, block_rows)
    (
        gain_one,
        shift_one,
        qbias_full,
        vbias_full,
        pbias_full,
        gain_two,
        shift_two,
        ubias_full,
        dbias_full,
    ) = gather_vectors(
        (
            first_gain,
            first_shift,
            query_bias,
            value_bias,
            proj_bias,
            second_gain,
            second_shift,
            up_bias,
            down_bias,
        )
    )
    qkv_full = lax.all_gather(qkv_weight, "dp", axis=0, tiled=True)
    proj_full = lax.all_gather(proj_weight, "dp", axis=0, tiled=True)
    up_full = lax.all_gather(up_weight, "dp", axis=0, tiled=True)
    down_full = lax.all_gather(down_weight, "dp", axis=0, tiled=True)
    inputs = tokens.reshape(total_rows, width).astype(jnp.float32)
    normed_one = layer_norm(inputs, gain_one, shift_one).astype(jnp.bfloat16)
    joined = jnp.dot(normed_one, qkv_full, preferred_element_type=jnp.float32)
    queries = ((joined[:, :width] + qbias_full) * scale).astype(jnp.bfloat16)
    keys = joined[:, width : 2 * width].astype(jnp.bfloat16).reshape(seq_count, local_rows, width)
    values = (
        (joined[:, 2 * width :] + vbias_full)
        .astype(jnp.bfloat16)
        .reshape(seq_count, local_rows, width)
    )
    query_heads = queries.reshape(seq_count, local_rows, head_count, head_size)

    def visible_mask(start, count):
        key_pos = block_positions(block_order, start, count, block_rows)
        return (query_pos[:, None] >= key_pos[None, :], jnp.min(key_pos))

    piece_keys = lax.all_gather(keys, "ctx", axis=1, tiled=True)
    piece_values = lax.all_gather(values, "ctx", axis=1, tiled=True)
    count = piece_keys.shape[1]
    visible, key_lowest = visible_mask(jnp.int32(0), count)
    seen = visible[None, :, None, :]
    row_max = jnp.full((seq_count, local_rows, head_count), neg_large, jnp.float32)
    key_heads = piece_keys.reshape(seq_count, count, head_count, head_size)
    value_heads = piece_values.reshape(seq_count, count, head_count, head_size)
    scores = jnp.einsum(
        "sqhd,skhd->sqhk", query_heads, key_heads, preferred_element_type=jnp.float32
    )
    scores = jnp.where(seen, scores, neg_large)
    new_max = jnp.maximum(row_max, jnp.max(scores, axis=-1))
    weights = jnp.where(seen, jnp.exp(scores - new_max[..., None]), 0.0)
    row_total = jnp.sum(weights, axis=-1)
    accum = jnp.einsum(
        "sqhk,skhd->sqhd",
        weights.astype(jnp.bfloat16),
        value_heads,
        preferred_element_type=jnp.float32,
    )
    result_state = (new_max, row_total, accum)
    row_max, row_total, accum = result_state
    attended_full = accum / row_total[..., None]
    log_total = row_max + jnp.log(row_total)
    attended = attended_full.reshape(total_rows, width).astype(jnp.bfloat16)
    branch = jnp.dot(attended, proj_full, preferred_element_type=jnp.float32) + pbias_full
    middle = inputs + branch
    normed_two = layer_norm(middle, gain_two, shift_two).astype(jnp.bfloat16)
    hidden = jnp.dot(normed_two, up_full, preferred_element_type=jnp.float32) + ubias_full
    active = gelu_tanh(hidden).astype(jnp.bfloat16)
    result = middle + jnp.dot(active, down_full, preferred_element_type=jnp.float32) + dbias_full
    output = result.astype(jnp.bfloat16).reshape(tokens.shape)
    up_back, down_back = up_full, down_full
    upstream = cotangent.reshape(total_rows, width)
    upstream_full = upstream.astype(jnp.float32)
    grad_down = jnp.einsum("rf,rd->fd", active, upstream, preferred_element_type=jnp.float32)
    grad_dbias = jnp.sum(upstream_full, axis=0)
    d_active = jnp.einsum("rd,fd->rf", upstream, down_back, preferred_element_type=jnp.float32)
    gelu_pull = jax.vjp(gelu_tanh, hidden)[1]
    d_hidden = gelu_pull(d_active)[0].astype(jnp.bfloat16)
    grad_up = jnp.einsum("rd,rf->df", normed_two, d_hidden, preferred_element_type=jnp.float32)
    grad_ubias = jnp.sum(d_hidden.astype(jnp.float32), axis=0)
    d_normed_two = jnp.einsum("rf,df->rd", d_hidden, up_back, preferred_element_type=jnp.float32)
    norm_pull_two = jax.vjp(layer_norm, middle, gain_two, shift_two)[1]
    d_middle_part, grad_gain_two, grad_shift_two = norm_pull_two(d_normed_two)
    d_middle = upstream_full + d_middle_part
    qkv_back, proj_back = qkv_full, proj_full
    d_branch = d_middle.astype(jnp.bfloat16)
    grad_proj = jnp.einsum("rd,re->de", attended, d_branch, preferred_element_type=jnp.float32)
    grad_pbias = jnp.sum(d_branch.astype(jnp.float32), axis=0)
    d_attended = jnp.einsum(
        "re,de->rd", d_branch, proj_back, preferred_element_type=jnp.float32
    ).astype(jnp.bfloat16)
    d_heads = d_attended.reshape(seq_count, local_rows, head_count, head_size)
    delta = jnp.sum(d_heads.astype(jnp.float32) * attended_full, axis=-1)
    piece_keys = lax.all_gather(keys, "ctx", axis=1, tiled=True)
    piece_values = lax.all_gather(values, "ctx", axis=1, tiled=True)
    count = piece_keys.shape[1]
    visible, key_lowest = visible_mask(jnp.int32(0), count)
    seen = visible[None, :, None, :]
    key_heads = piece_keys.reshape(seq_count, count, head_count, head_size)
    value_heads = piece_values.reshape(seq_count, count, head_count, head_size)
    scores = jnp.einsum(
        "sqhd,skhd->sqhk", query_heads, key_heads, preferred_element_type=jnp.float32
    )
    weights = jnp.where(seen, jnp.exp(scores - log_total[..., None]), 0.0)
    d_weights = jnp.einsum(
        "sqhd,skhd->sqhk", d_heads, value_heads, preferred_element_type=jnp.float32
    )
    d_scores = (weights * (d_weights - delta[..., None])).astype(jnp.bfloat16)
    d_query = jnp.einsum("sqhk,skhd->sqhd", d_scores, key_heads, preferred_element_type=jnp.float32)
    d_key = jnp.einsum(
        "sqhk,sqhd->skhd", d_scores, query_heads, preferred_element_type=jnp.float32
    ).reshape(seq_count, count, width)
    d_value = jnp.einsum(
        "sqhk,sqhd->skhd", weights.astype(jnp.bfloat16), d_heads, preferred_element_type=jnp.float32
    ).reshape(seq_count, count, width)
    d_key_all = d_key
    d_value_all = d_value
    result_state = (d_query, d_key_all, d_value_all)
    d_query, d_key_all, d_value_all = result_state
    d_key_sum, d_value_sum = (
        lax.psum_scatter(
            d_key_all.astype(jnp.bfloat16), "ctx", scatter_dimension=1, tiled=True
        ).astype(jnp.float32),
        lax.psum_scatter(
            d_value_all.astype(jnp.bfloat16), "ctx", scatter_dimension=1, tiled=True
        ).astype(jnp.float32),
    )
    d_queries = d_query.reshape(total_rows, width).astype(jnp.bfloat16) * scale
    d_keys = d_key_sum.reshape(total_rows, width).astype(jnp.bfloat16)
    d_values = d_value_sum.reshape(total_rows, width).astype(jnp.bfloat16)
    d_joined = jnp.concatenate((d_queries, d_keys, d_values), axis=1)
    grad_parts = [
        jnp.einsum("rd,re->de", normed_one, part, preferred_element_type=jnp.float32)
        for part in (d_queries, d_keys, d_values)
    ]
    grad_qbias = jnp.sum(d_queries.astype(jnp.float32), axis=0)
    grad_vbias = jnp.sum(d_values.astype(jnp.float32), axis=0)
    d_normed_one = jnp.einsum("re,de->rd", d_joined, qkv_back, preferred_element_type=jnp.float32)
    norm_pull_one = jax.vjp(layer_norm, inputs, gain_one, shift_one)[1]
    d_inputs, grad_gain_one, grad_shift_one = norm_pull_one(d_normed_one)
    grad_tokens = (d_middle + d_inputs).astype(jnp.bfloat16).reshape(tokens.shape)
    shaped_qkv = jnp.concatenate(
        [reduce_matrix(grad_parts[number], number == 2) for number in range(3)], axis=1
    )
    shaped_proj = reduce_matrix(grad_proj, True)
    shaped_up = reduce_matrix(grad_up, True)
    shaped_down = reduce_matrix(grad_down, False)
    early = reduce_vectors(
        (grad_pbias, grad_gain_two, grad_shift_two, grad_ubias, grad_dbias)
    )
    late = reduce_vectors((grad_gain_one, grad_shift_one, grad_qbias, grad_vbias))
    return (
        output,
        grad_tokens,
        late[0],
        late[1],
        shaped_qkv,
        late[2],
        late[3],
        shaped_proj,
        early[0],
        early[1],
        early[2],
        shaped_up,
        early[3],
        shaped_down,
        early[4],
    )


def solution(mesh):
    return jax.shard_map(
        per_device,
        mesh=mesh,
        in_specs=(
            P("dp", "ctx", None),
            P("dp"),
            P("dp"),
            P("dp", None),
            P("dp"),
            P("dp"),
            P("dp", None),
            P("dp"),
            P("dp"),
            P("dp"),
            P("dp", None),
            P("dp"),
            P("dp", None),
            P("dp"),
            P(),
            P("dp", "ctx", None),
        ),
        out_specs=(
            P("dp", "ctx", None),
            P("dp", "ctx", None),
            P("dp"),
            P("dp"),
            P("dp", None),
            P("dp"),
            P("dp"),
            P("dp", None),
            P("dp"),
            P("dp"),
            P("dp"),
            P("dp", None),
            P("dp"),
            P("dp", None),
            P("dp"),
        ),
        check_vma=False,
    )
```

```python
import math

import jax
import jax.numpy as jnp
from jax import lax
from jax.sharding import PartitionSpec as P

HEADS = 17


eps = 1e-05
neg_large = -1e30


def layer_norm(values, norm_gain, norm_shift):
    average = jnp.mean(values, axis=-1, keepdims=True)
    centered = values - average
    spread = jnp.mean(centered * centered, axis=-1, keepdims=True)
    return centered * lax.rsqrt(spread + eps) * norm_gain + norm_shift


def gelu_tanh(values):
    return jax.nn.gelu(values, approximate=True)


def block_positions(block_order, first_row, count, block_rows):
    row_index = first_row + jnp.arange(count, dtype=jnp.int32)
    row_index = row_index % (block_order.shape[0] * block_rows)
    block_index = row_index // block_rows
    numbers = jnp.arange(block_order.shape[0], dtype=jnp.int32)
    picked = jnp.sum(
        jnp.where(block_index[:, None] == numbers[None, :], block_order[None, :], 0), axis=1
    )
    return picked * block_rows + row_index % block_rows


def swap(values, axis, bit):
    count = lax.axis_size(axis)
    return lax.ppermute(values, axis, [(i, i ^ (1 << bit)) for i in range(count)])


def bit_of(axis, bit):
    return (lax.axis_index(axis) >> bit) & 1


def bits_in(axis):
    return lax.axis_size(axis).bit_length() - 1


def halve_steps(parts, axis, order, wire):
    left = list(range(bits_in(axis)))
    for bit in order:
        low = 1 << left.index(bit)
        left.remove(bit)
        rest = parts.shape[1:]
        view = parts.reshape((parts.shape[0] // (2 * low), 2, low) + rest)
        mine = bit_of(axis, bit)
        sent = lax.dynamic_index_in_dim(view, 1 - mine, 1, keepdims=False).astype(wire)
        kept = lax.dynamic_index_in_dim(view, mine, 1, keepdims=False)
        yield sent
        total = kept.astype(jnp.float32) + swap(sent, axis, bit).astype(jnp.float32)
        parts = total.astype(wire).reshape((-1,) + rest)
    return parts[0]


def finish(steps):
    while True:
        try:
            next(steps)
        except StopIteration as stop:
            return stop.value


def tie(value, *others):
    return lax.optimization_barrier((value,) + others)[0]


def ring_gather(values, axis):
    count = lax.axis_size(axis)
    place = lax.axis_index(axis)
    lower, upper = [values], [values]
    for step in range(1, count):
        lower.append(lax.ppermute(lower[-1], axis, [(i, i + 1) for i in range(step - 1, count - 1)]))
        upper.append(lax.ppermute(upper[-1], axis, [(i + 1, i) for i in range(count - step)]))
    blocks = [values]
    for step in range(1, count):
        blocks.append(jnp.where(place + step < count, upper[step], lower[count - step]))
    return jnp.concatenate(blocks, axis=1)


def double(piece, axis, order):
    have = []
    parts = piece[None]
    for bit in order:
        low = 1 << sum(1 for other in have if other < bit)
        have.append(bit)
        rest = parts.shape[1:]
        other = swap(parts, axis, bit)
        mine = bit_of(axis, bit) == 1
        first = jnp.where(mine, other, parts)
        second = jnp.where(mine, parts, other)
        high = parts.shape[0] // low
        pair = jnp.stack(
            (first.reshape((high, low) + rest), second.reshape((high, low) + rest)), axis=1
        )
        parts = pair.reshape((-1,) + rest)
    return parts


def reduce_steps(grad, flip):
    dp_count, ctx_count = lax.axis_size("dp"), lax.axis_size("ctx")
    rows, columns = grad.shape
    order = list(range(bits_in("dp")))
    if flip:
        order = order[:1] + order[:0:-1]
    own = rows // dp_count
    shard = yield from halve_steps(
        grad.reshape(dp_count, own, columns), "dp", order, jnp.bfloat16
    )
    order = list(range(bits_in("ctx")))
    extra = -own % ctx_count
    if extra:
        shard = jnp.pad(shard, ((0, extra), (0, 0)))
    piece = yield from halve_steps(
        shard.reshape(ctx_count, -1, columns), "ctx", order, jnp.bfloat16
    )
    gathered = double(piece, "ctx", order[::-1]).reshape(-1, columns)
    return gathered[:own].astype(jnp.float32)


def reduce_vectors(grads):
    dp_count = lax.axis_size("dp")
    parts = jnp.concatenate([grad.reshape(dp_count, -1) for grad in grads], axis=1)
    total = finish(halve_steps(parts, "dp", list(range(bits_in("dp"))), jnp.float32))
    for bit in range(bits_in("ctx")):
        total = total + swap(total, "ctx", bit)
    sizes = [grad.shape[0] // dp_count for grad in grads]
    return jnp.split(total, [sum(sizes[: i + 1]) for i in range(len(sizes) - 1)])


def gather_vectors(shards):
    joined = jnp.concatenate(shards).astype(jnp.float32)
    parts = double(joined, "dp", list(range(bits_in("dp"))))
    sizes = [shard.shape[0] for shard in shards]
    pieces = jnp.split(parts, [sum(sizes[: i + 1]) for i in range(len(sizes) - 1)], axis=1)
    return [piece.reshape(-1) for piece in pieces]


def per_device(
    tokens,
    first_gain,
    first_shift,
    qkv_weight,
    query_bias,
    value_bias,
    proj_weight,
    proj_bias,
    second_gain,
    second_shift,
    up_weight,
    up_bias,
    down_weight,
    down_bias,
    block_order,
    cotangent,
):
    seq_count, local_rows, width = tokens.shape
    head_count = HEADS
    head_size = width // head_count
    scale = 1.0 / math.sqrt(head_size)
    block_rows = local_rows // 2
    total_rows = seq_count * local_rows
    place_index = lax.axis_index("ctx")
    query_pos = block_positions(block_order, place_index * local_rows, local_rows, block_rows)
    (
        gain_one,
        shift_one,
        qbias_full,
        vbias_full,
        pbias_full,
        gain_two,
        shift_two,
        ubias_full,
        dbias_full,
    ) = gather_vectors(
        (
            first_gain,
            first_shift,
            query_bias,
            value_bias,
            proj_bias,
            second_gain,
            second_shift,
            up_bias,
            down_bias,
        )
    )
    qkv_full = lax.all_gather(qkv_weight, "dp", axis=0, tiled=True)
    proj_full = lax.all_gather(proj_weight, "dp", axis=0, tiled=True)
    up_full = lax.all_gather(up_weight, "dp", axis=0, tiled=True)
    down_full = lax.all_gather(down_weight, "dp", axis=0, tiled=True)
    inputs = tokens.reshape(total_rows, width).astype(jnp.float32)
    normed_one = layer_norm(inputs, gain_one, shift_one).astype(jnp.bfloat16)
    joined = jnp.dot(normed_one, qkv_full, preferred_element_type=jnp.float32)
    queries = ((joined[:, :width] + qbias_full) * scale).astype(jnp.bfloat16)
    keys = joined[:, width : 2 * width].astype(jnp.bfloat16).reshape(seq_count, local_rows, width)
    values = (
        (joined[:, 2 * width :] + vbias_full)
        .astype(jnp.bfloat16)
        .reshape(seq_count, local_rows, width)
    )
    query_heads = queries.reshape(seq_count, local_rows, head_count, head_size)

    def visible_mask(start, count):
        key_pos = block_positions(block_order, start, count, block_rows)
        return (query_pos[:, None] >= key_pos[None, :], jnp.min(key_pos))

    piece_keys = ring_gather(keys, "ctx")
    piece_values = ring_gather(tie(values, piece_keys), "ctx")
    piece_keys = tie(piece_keys, proj_full)
    count = piece_keys.shape[1]
    visible, key_lowest = visible_mask(place_index * local_rows, count)
    seen = visible[None, :, None, :]
    row_max = jnp.full((seq_count, local_rows, head_count), neg_large, jnp.float32)
    key_heads = piece_keys.reshape(seq_count, count, head_count, head_size)
    value_heads = piece_values.reshape(seq_count, count, head_count, head_size)
    scores = jnp.einsum(
        "sqhd,skhd->sqhk", query_heads, key_heads, preferred_element_type=jnp.float32
    )
    scores = jnp.where(seen, scores, neg_large)
    new_max = jnp.maximum(row_max, jnp.max(scores, axis=-1))
    weights = jnp.where(seen, jnp.exp(scores - new_max[..., None]), 0.0)
    row_total = jnp.sum(weights, axis=-1)
    value_heads = tie(value_heads, up_full)
    accum = jnp.einsum(
        "sqhk,skhd->sqhd",
        weights.astype(jnp.bfloat16),
        value_heads,
        preferred_element_type=jnp.float32,
    )
    result_state = (new_max, row_total, accum)
    row_max, row_total, accum = result_state
    attended_full = accum / row_total[..., None]
    log_total = row_max + jnp.log(row_total)
    attended = attended_full.reshape(total_rows, width).astype(jnp.bfloat16)
    attended = tie(attended, down_full)
    branch = jnp.dot(attended, proj_full, preferred_element_type=jnp.float32) + pbias_full
    middle = inputs + branch
    normed_two = layer_norm(middle, gain_two, shift_two).astype(jnp.bfloat16)
    hidden = jnp.dot(normed_two, up_full, preferred_element_type=jnp.float32) + ubias_full
    active = gelu_tanh(hidden).astype(jnp.bfloat16)
    result = middle + jnp.dot(active, down_full, preferred_element_type=jnp.float32) + dbias_full
    output = result.astype(jnp.bfloat16).reshape(tokens.shape)
    up_back, down_back = up_full, down_full
    upstream = cotangent.reshape(total_rows, width)
    upstream_full = upstream.astype(jnp.float32)
    grad_down = jnp.einsum("rf,rd->fd", active, upstream, preferred_element_type=jnp.float32)
    grad_dbias = jnp.sum(upstream_full, axis=0)
    d_active = jnp.einsum("rd,fd->rf", upstream, down_back, preferred_element_type=jnp.float32)
    gelu_pull = jax.vjp(gelu_tanh, hidden)[1]
    d_hidden = gelu_pull(d_active)[0].astype(jnp.bfloat16)
    grad_up = jnp.einsum("rd,rf->df", normed_two, d_hidden, preferred_element_type=jnp.float32)
    grad_ubias = jnp.sum(d_hidden.astype(jnp.float32), axis=0)
    d_normed_two = jnp.einsum("rf,df->rd", d_hidden, up_back, preferred_element_type=jnp.float32)
    norm_pull_two = jax.vjp(layer_norm, middle, gain_two, shift_two)[1]
    d_middle_part, grad_gain_two, grad_shift_two = norm_pull_two(d_normed_two)
    d_middle = upstream_full + d_middle_part
    qkv_back, proj_back = qkv_full, proj_full
    d_branch = d_middle.astype(jnp.bfloat16)
    grad_proj = jnp.einsum("rd,re->de", attended, d_branch, preferred_element_type=jnp.float32)
    grad_pbias = jnp.sum(d_branch.astype(jnp.float32), axis=0)
    d_attended = jnp.einsum(
        "re,de->rd", d_branch, proj_back, preferred_element_type=jnp.float32
    ).astype(jnp.bfloat16)
    d_heads = d_attended.reshape(seq_count, local_rows, head_count, head_size)
    delta = jnp.sum(d_heads.astype(jnp.float32) * attended_full, axis=-1)
    running = [reduce_steps(grad_down, False), reduce_steps(grad_up, True), reduce_steps(grad_proj, True)]

    def after_exchange(value):
        return tie(value, *[next(steps) for steps in running])

    seen = visible[None, :, None, :]
    key_heads = after_exchange(piece_keys).reshape(seq_count, count, head_count, head_size)
    scores = jnp.einsum(
        "sqhd,skhd->sqhk", query_heads, key_heads, preferred_element_type=jnp.float32
    )
    weights = jnp.where(seen, jnp.exp(scores - log_total[..., None]), 0.0)
    value_heads = after_exchange(piece_values).reshape(seq_count, count, head_count, head_size)
    d_weights = jnp.einsum(
        "sqhd,skhd->sqhk", d_heads, value_heads, preferred_element_type=jnp.float32
    )
    d_scores = (weights * (d_weights - delta[..., None])).astype(jnp.bfloat16)
    d_heads = after_exchange(d_heads)
    d_value = jnp.einsum(
        "sqhk,sqhd->skhd", weights.astype(jnp.bfloat16), d_heads, preferred_element_type=jnp.float32
    ).reshape(seq_count, count, width)
    d_key = jnp.einsum(
        "sqhk,sqhd->skhd", d_scores, query_heads, preferred_element_type=jnp.float32
    ).reshape(seq_count, count, width)
    d_value = jnp.roll(d_value.astype(jnp.bfloat16), place_index * local_rows, axis=1)
    d_key = jnp.roll(d_key.astype(jnp.bfloat16), place_index * local_rows, axis=1)
    key_heads = after_exchange(key_heads)
    d_query = jnp.einsum("sqhk,skhd->sqhd", d_scores, key_heads, preferred_element_type=jnp.float32)
    d_key_all = d_key
    d_value_all = d_value
    result_state = (d_query, d_key_all, d_value_all)
    d_query, d_key_all, d_value_all = result_state
    d_key_sum, d_value_sum = (
        lax.psum_scatter(
            d_key_all.astype(jnp.bfloat16), "ctx", scatter_dimension=1, tiled=True
        ).astype(jnp.float32),
        lax.psum_scatter(
            d_value_all.astype(jnp.bfloat16), "ctx", scatter_dimension=1, tiled=True
        ).astype(jnp.float32),
    )
    d_queries = d_query.reshape(total_rows, width).astype(jnp.bfloat16) * scale
    d_keys = d_key_sum.reshape(total_rows, width).astype(jnp.bfloat16)
    d_values = d_value_sum.reshape(total_rows, width).astype(jnp.bfloat16)
    d_joined = jnp.concatenate((d_queries, d_keys, d_values), axis=1)
    grad_parts = [
        jnp.einsum("rd,re->de", normed_one, part, preferred_element_type=jnp.float32)
        for part in (d_queries, d_keys, d_values)
    ]
    grad_qbias = jnp.sum(d_queries.astype(jnp.float32), axis=0)
    grad_vbias = jnp.sum(d_values.astype(jnp.float32), axis=0)
    d_normed_one = jnp.einsum("re,de->rd", d_joined, qkv_back, preferred_element_type=jnp.float32)
    norm_pull_one = jax.vjp(layer_norm, inputs, gain_one, shift_one)[1]
    d_inputs, grad_gain_one, grad_shift_one = norm_pull_one(d_normed_one)
    grad_tokens = (d_middle + d_inputs).astype(jnp.bfloat16).reshape(tokens.shape)
    shaped_qkv = jnp.concatenate(
        [finish(reduce_steps(grad_parts[number], number == 2)) for number in range(3)], axis=1
    )
    shaped_down, shaped_up, shaped_proj = [finish(steps) for steps in running]
    early = reduce_vectors(
        (grad_pbias, grad_gain_two, grad_shift_two, grad_ubias, grad_dbias)
    )
    late = reduce_vectors((grad_gain_one, grad_shift_one, grad_qbias, grad_vbias))
    return (
        output,
        grad_tokens,
        late[0],
        late[1],
        shaped_qkv,
        late[2],
        late[3],
        shaped_proj,
        early[0],
        early[1],
        early[2],
        shaped_up,
        early[3],
        shaped_down,
        early[4],
    )


def solution(mesh):
    return jax.shard_map(
        per_device,
        mesh=mesh,
        in_specs=(
            P("dp", "ctx", None),
            P("dp"),
            P("dp"),
            P("dp", None),
            P("dp"),
            P("dp"),
            P("dp", None),
            P("dp"),
            P("dp"),
            P("dp"),
            P("dp", None),
            P("dp"),
            P("dp", None),
            P("dp"),
            P(),
            P("dp", "ctx", None),
        ),
        out_specs=(
            P("dp", "ctx", None),
            P("dp", "ctx", None),
            P("dp"),
            P("dp"),
            P("dp", None),
            P("dp"),
            P("dp"),
            P("dp", None),
            P("dp"),
            P("dp"),
            P("dp"),
            P("dp", None),
            P("dp"),
            P("dp", None),
            P("dp"),
        ),
        check_vma=False,
    )
```

```python
import math

import jax
import jax.numpy as jnp
from jax import lax
from jax.sharding import PartitionSpec as P

HEADS = 17


eps = 1e-05
neg_large = -1e30


def layer_norm(values, norm_gain, norm_shift):
    average = jnp.mean(values, axis=-1, keepdims=True)
    centered = values - average
    spread = jnp.mean(centered * centered, axis=-1, keepdims=True)
    return centered * lax.rsqrt(spread + eps) * norm_gain + norm_shift


def gelu_tanh(values):
    return jax.nn.gelu(values, approximate=True)


def block_positions(block_order, first_row, count, block_rows):
    row_index = first_row + jnp.arange(count, dtype=jnp.int32)
    row_index = row_index % (block_order.shape[0] * block_rows)
    block_index = row_index // block_rows
    numbers = jnp.arange(block_order.shape[0], dtype=jnp.int32)
    picked = jnp.sum(
        jnp.where(block_index[:, None] == numbers[None, :], block_order[None, :], 0), axis=1
    )
    return picked * block_rows + row_index % block_rows


def swap(values, axis, bit):
    count = lax.axis_size(axis)
    return lax.ppermute(values, axis, [(i, i ^ (1 << bit)) for i in range(count)])


def bit_of(axis, bit):
    return (lax.axis_index(axis) >> bit) & 1


def bits_in(axis):
    return lax.axis_size(axis).bit_length() - 1


def halve_steps(parts, axis, order, wire):
    left = list(range(bits_in(axis)))
    for bit in order:
        low = 1 << left.index(bit)
        left.remove(bit)
        rest = parts.shape[1:]
        view = parts.reshape((parts.shape[0] // (2 * low), 2, low) + rest)
        mine = bit_of(axis, bit)
        sent = lax.dynamic_index_in_dim(view, 1 - mine, 1, keepdims=False).astype(wire)
        kept = lax.dynamic_index_in_dim(view, mine, 1, keepdims=False)
        after = yield sent
        if after is not None:
            sent = tie(sent, after)
        total = kept.astype(jnp.float32) + swap(sent, axis, bit).astype(jnp.float32)
        parts = total.astype(wire).reshape((-1,) + rest)
    return parts[0]


def finish(steps):
    while True:
        try:
            next(steps)
        except StopIteration as stop:
            return stop.value


def tie(value, *others):
    return lax.optimization_barrier((value,) + others)[0]


def ring_gather(values, axis):
    count = lax.axis_size(axis)
    place = lax.axis_index(axis)
    lower, upper = [values], [values]
    for step in range(1, count):
        lower.append(lax.ppermute(lower[-1], axis, [(i, i + 1) for i in range(step - 1, count - 1)]))
        upper.append(lax.ppermute(upper[-1], axis, [(i + 1, i) for i in range(count - step)]))
    blocks = [values]
    for step in range(1, count):
        blocks.append(jnp.where(place + step < count, upper[step], lower[count - step]))
    return jnp.concatenate(blocks, axis=1)


def double(piece, axis, order):
    have = []
    parts = piece[None]
    for bit in order:
        low = 1 << sum(1 for other in have if other < bit)
        have.append(bit)
        rest = parts.shape[1:]
        other = swap(parts, axis, bit)
        mine = bit_of(axis, bit) == 1
        first = jnp.where(mine, other, parts)
        second = jnp.where(mine, parts, other)
        high = parts.shape[0] // low
        pair = jnp.stack(
            (first.reshape((high, low) + rest), second.reshape((high, low) + rest)), axis=1
        )
        parts = pair.reshape((-1,) + rest)
    return parts


def reduce_steps(grad, flip):
    dp_count, ctx_count = lax.axis_size("dp"), lax.axis_size("ctx")
    rows, columns = grad.shape
    order = list(range(bits_in("dp")))
    if flip:
        order = order[:1] + order[:0:-1]
    own = rows // dp_count
    shard = yield from halve_steps(
        grad.reshape(dp_count, own, columns), "dp", order, jnp.bfloat16
    )
    order = list(range(bits_in("ctx")))
    extra = -own % ctx_count
    if extra:
        shard = jnp.pad(shard, ((0, extra), (0, 0)))
    piece = yield from halve_steps(
        shard.reshape(ctx_count, -1, columns), "ctx", order, jnp.bfloat16
    )
    gathered = double(piece, "ctx", order[::-1]).reshape(-1, columns)
    return gathered[:own].astype(jnp.float32)


def reduce_vectors(grads):
    dp_count = lax.axis_size("dp")
    parts = jnp.concatenate([grad.reshape(dp_count, -1) for grad in grads], axis=1)
    total = finish(halve_steps(parts, "dp", list(range(bits_in("dp"))), jnp.float32))
    for bit in range(bits_in("ctx")):
        total = total + swap(total, "ctx", bit)
    sizes = [grad.shape[0] // dp_count for grad in grads]
    return jnp.split(total, [sum(sizes[: i + 1]) for i in range(len(sizes) - 1)])


def gather_vectors(shards):
    joined = jnp.concatenate(shards).astype(jnp.float32)
    parts = double(joined, "dp", list(range(bits_in("dp"))))
    sizes = [shard.shape[0] for shard in shards]
    pieces = jnp.split(parts, [sum(sizes[: i + 1]) for i in range(len(sizes) - 1)], axis=1)
    return [piece.reshape(-1) for piece in pieces]


def per_device(
    tokens,
    first_gain,
    first_shift,
    qkv_weight,
    query_bias,
    value_bias,
    proj_weight,
    proj_bias,
    second_gain,
    second_shift,
    up_weight,
    up_bias,
    down_weight,
    down_bias,
    block_order,
    cotangent,
):
    seq_count, local_rows, width = tokens.shape
    head_count = HEADS
    head_size = width // head_count
    scale = 1.0 / math.sqrt(head_size)
    block_rows = local_rows // 2
    total_rows = seq_count * local_rows
    place_index = lax.axis_index("ctx")
    query_pos = block_positions(block_order, place_index * local_rows, local_rows, block_rows)
    (
        gain_one,
        shift_one,
        qbias_full,
        vbias_full,
        pbias_full,
        gain_two,
        shift_two,
        ubias_full,
        dbias_full,
    ) = gather_vectors(
        (
            first_gain,
            first_shift,
            query_bias,
            value_bias,
            proj_bias,
            second_gain,
            second_shift,
            up_bias,
            down_bias,
        )
    )
    qkv_full = lax.all_gather(qkv_weight, "dp", axis=0, tiled=True)
    proj_full = lax.all_gather(proj_weight, "dp", axis=0, tiled=True)
    up_full = lax.all_gather(up_weight, "dp", axis=0, tiled=True)
    down_full = lax.all_gather(down_weight, "dp", axis=0, tiled=True)
    inputs = tokens.reshape(total_rows, width).astype(jnp.float32)
    normed_one = layer_norm(inputs, gain_one, shift_one).astype(jnp.bfloat16)
    joined = jnp.dot(normed_one, qkv_full, preferred_element_type=jnp.float32)
    queries = ((joined[:, :width] + qbias_full) * scale).astype(jnp.bfloat16)
    keys = joined[:, width : 2 * width].astype(jnp.bfloat16).reshape(seq_count, local_rows, width)
    values = (
        (joined[:, 2 * width :] + vbias_full)
        .astype(jnp.bfloat16)
        .reshape(seq_count, local_rows, width)
    )
    query_heads = queries.reshape(seq_count, local_rows, head_count, head_size)

    def visible_mask(start, count):
        key_pos = block_positions(block_order, start, count, block_rows)
        return (query_pos[:, None] >= key_pos[None, :], jnp.min(key_pos))

    piece_keys = ring_gather(keys, "ctx")
    piece_values = ring_gather(tie(values, piece_keys), "ctx")
    piece_keys = tie(piece_keys, proj_full)
    count = piece_keys.shape[1]
    visible, key_lowest = visible_mask(place_index * local_rows, count)
    seen = visible[None, :, None, :]
    row_max = jnp.full((seq_count, local_rows, head_count), neg_large, jnp.float32)
    key_heads = piece_keys.reshape(seq_count, count, head_count, head_size)
    value_heads = piece_values.reshape(seq_count, count, head_count, head_size)
    scores = jnp.einsum(
        "sqhd,skhd->sqhk", query_heads, key_heads, preferred_element_type=jnp.float32
    )
    scores = jnp.where(seen, scores, neg_large)
    new_max = jnp.maximum(row_max, jnp.max(scores, axis=-1))
    weights = jnp.where(seen, jnp.exp(scores - new_max[..., None]), 0.0)
    row_total = jnp.sum(weights, axis=-1)
    value_heads = tie(value_heads, up_full)
    accum = jnp.einsum(
        "sqhk,skhd->sqhd",
        weights.astype(jnp.bfloat16),
        value_heads,
        preferred_element_type=jnp.float32,
    )
    result_state = (new_max, row_total, accum)
    row_max, row_total, accum = result_state
    attended_full = accum / row_total[..., None]
    log_total = row_max + jnp.log(row_total)
    attended = attended_full.reshape(total_rows, width).astype(jnp.bfloat16)
    attended = tie(attended, down_full)
    branch = jnp.dot(attended, proj_full, preferred_element_type=jnp.float32) + pbias_full
    middle = inputs + branch
    normed_two = layer_norm(middle, gain_two, shift_two).astype(jnp.bfloat16)
    hidden = jnp.dot(normed_two, up_full, preferred_element_type=jnp.float32) + ubias_full
    active = gelu_tanh(hidden).astype(jnp.bfloat16)
    result = middle + jnp.dot(active, down_full, preferred_element_type=jnp.float32) + dbias_full
    output = result.astype(jnp.bfloat16).reshape(tokens.shape)
    up_back, down_back = up_full, down_full
    upstream = cotangent.reshape(total_rows, width)
    upstream_full = upstream.astype(jnp.float32)
    grad_down = jnp.einsum("rf,rd->fd", active, upstream, preferred_element_type=jnp.float32)
    grad_dbias = jnp.sum(upstream_full, axis=0)
    d_active = jnp.einsum("rd,fd->rf", upstream, down_back, preferred_element_type=jnp.float32)
    gelu_pull = jax.vjp(gelu_tanh, hidden)[1]
    d_hidden = gelu_pull(d_active)[0].astype(jnp.bfloat16)
    grad_up = jnp.einsum("rd,rf->df", normed_two, d_hidden, preferred_element_type=jnp.float32)
    grad_ubias = jnp.sum(d_hidden.astype(jnp.float32), axis=0)
    d_normed_two = jnp.einsum("rf,df->rd", d_hidden, up_back, preferred_element_type=jnp.float32)
    norm_pull_two = jax.vjp(layer_norm, middle, gain_two, shift_two)[1]
    d_middle_part, grad_gain_two, grad_shift_two = norm_pull_two(d_normed_two)
    d_middle = upstream_full + d_middle_part
    qkv_back, proj_back = qkv_full, proj_full
    d_branch = d_middle.astype(jnp.bfloat16)
    grad_proj = jnp.einsum("rd,re->de", attended, d_branch, preferred_element_type=jnp.float32)
    grad_pbias = jnp.sum(d_branch.astype(jnp.float32), axis=0)
    d_attended = jnp.einsum(
        "re,de->rd", d_branch, proj_back, preferred_element_type=jnp.float32
    ).astype(jnp.bfloat16)
    d_heads = d_attended.reshape(seq_count, local_rows, head_count, head_size)
    delta = jnp.sum(d_heads.astype(jnp.float32) * attended_full, axis=-1)
    running = [reduce_steps(grad_down, False), reduce_steps(grad_up, True), reduce_steps(grad_proj, True)]

    def after_exchange(value):
        return tie(value, *[next(steps) for steps in running])

    seen = visible[None, :, None, :]
    key_heads = after_exchange(piece_keys).reshape(seq_count, count, head_count, head_size)
    scores = jnp.einsum(
        "sqhd,skhd->sqhk", query_heads, key_heads, preferred_element_type=jnp.float32
    )
    weights = jnp.where(seen, jnp.exp(scores - log_total[..., None]), 0.0)
    d_heads = after_exchange(d_heads)
    d_value = jnp.einsum(
        "sqhk,sqhd->skhd", weights.astype(jnp.bfloat16), d_heads, preferred_element_type=jnp.float32
    ).reshape(seq_count, count, width)
    d_value = jnp.roll(d_value.astype(jnp.bfloat16), place_index * local_rows, axis=1)
    value_heads = tie(piece_values, d_value).reshape(seq_count, count, head_count, head_size)
    d_weights = jnp.einsum(
        "sqhd,skhd->sqhk", d_heads, value_heads, preferred_element_type=jnp.float32
    )
    d_scores = (weights * (d_weights - delta[..., None])).astype(jnp.bfloat16)
    query_heads = after_exchange(query_heads)
    d_key = jnp.einsum(
        "sqhk,sqhd->skhd", d_scores, query_heads, preferred_element_type=jnp.float32
    ).reshape(seq_count, count, width)
    d_key = jnp.roll(d_key.astype(jnp.bfloat16), place_index * local_rows, axis=1)
    key_heads = tie(key_heads, d_key)
    d_query = jnp.einsum("sqhk,skhd->sqhd", d_scores, key_heads, preferred_element_type=jnp.float32)
    d_key_all = d_key
    d_value_all = d_value
    result_state = (d_query, d_key_all, d_value_all)
    d_query, d_key_all, d_value_all = result_state
    d_key_sum, d_value_sum = (
        lax.psum_scatter(
            d_key_all.astype(jnp.bfloat16), "ctx", scatter_dimension=1, tiled=True
        ).astype(jnp.float32),
        lax.psum_scatter(
            d_value_all.astype(jnp.bfloat16), "ctx", scatter_dimension=1, tiled=True
        ).astype(jnp.float32),
    )
    for steps in running:
        next(steps)
        steps.send(d_key_sum)
    d_queries = d_query.reshape(total_rows, width).astype(jnp.bfloat16) * scale
    d_keys = d_key_sum.reshape(total_rows, width).astype(jnp.bfloat16)
    d_values = d_value_sum.reshape(total_rows, width).astype(jnp.bfloat16)
    d_joined = jnp.concatenate((d_queries, d_keys, d_values), axis=1)
    grad_parts = [
        jnp.einsum("rd,re->de", normed_one, part, preferred_element_type=jnp.float32)
        for part in (d_queries, d_keys, d_values)
    ]
    grad_qbias = jnp.sum(d_queries.astype(jnp.float32), axis=0)
    grad_vbias = jnp.sum(d_values.astype(jnp.float32), axis=0)
    d_normed_one = jnp.einsum("re,de->rd", d_joined, qkv_back, preferred_element_type=jnp.float32)
    norm_pull_one = jax.vjp(layer_norm, inputs, gain_one, shift_one)[1]
    d_inputs, grad_gain_one, grad_shift_one = norm_pull_one(d_normed_one)
    grad_tokens = (d_middle + d_inputs).astype(jnp.bfloat16).reshape(tokens.shape)
    shaped_qkv = jnp.concatenate(
        [finish(reduce_steps(grad_parts[number], number == 2)) for number in range(3)], axis=1
    )
    shaped_down, shaped_up, shaped_proj = [finish(steps) for steps in running]
    early = reduce_vectors(
        (grad_pbias, grad_gain_two, grad_shift_two, grad_ubias, grad_dbias)
    )
    late = reduce_vectors((grad_gain_one, grad_shift_one, grad_qbias, grad_vbias))
    return (
        output,
        grad_tokens,
        late[0],
        late[1],
        shaped_qkv,
        late[2],
        late[3],
        shaped_proj,
        early[0],
        early[1],
        early[2],
        shaped_up,
        early[3],
        shaped_down,
        early[4],
    )


def solution(mesh):
    return jax.shard_map(
        per_device,
        mesh=mesh,
        in_specs=(
            P("dp", "ctx", None),
            P("dp"),
            P("dp"),
            P("dp", None),
            P("dp"),
            P("dp"),
            P("dp", None),
            P("dp"),
            P("dp"),
            P("dp"),
            P("dp", None),
            P("dp"),
            P("dp", None),
            P("dp"),
            P(),
            P("dp", "ctx", None),
        ),
        out_specs=(
            P("dp", "ctx", None),
            P("dp", "ctx", None),
            P("dp"),
            P("dp"),
            P("dp", None),
            P("dp"),
            P("dp"),
            P("dp", None),
            P("dp"),
            P("dp"),
            P("dp"),
            P("dp", None),
            P("dp"),
            P("dp", None),
            P("dp"),
        ),
        check_vma=False,
    )
```
